32 devices in a mesh: doc: 8 (over z, x), vocab: 4 (over y, core).
Axes of the slice: x: 2, y: 2, z: 4, core: 2. Of those that a mesh axis runs over, the one named last changes fastest.
Arguments:
- count_tiles: int32 [32, 32, 2, 16, 128], P(('doc', 'vocab')), may hold values from 0 to 3
- tile_words: int32 [32, 32, 2], P(('doc', 'vocab')), may hold values from 0 to 31
- whitening: bfloat16 [131072, 512], P(('doc', 'vocab')), may hold values from -0.08 to 0.16
- seeds: int32 [512], replicated, may hold values from 0 to 511, as said below
Outputs:
- topic_directions: float32 [512, 512], P('vocab')
- topic_weights: float32 [512], replicated
The draws below stay inside these ranges and needn't reach their ends.
Inputs may be any that keep to these rules, and one draw needn't show every extreme that they name: `seeds`: 512 distinct document indices; the first and the last document are among them.
All inputs are finite; a program needn't handle non-finite values.
Results may differ from the reference program's by a relative error of at most 0.0003.
Values sent between devices are 32-bit elements; how exact they have to be, the bound alone decides.
No kernel may reach another device: no remote copies, remote signals or barrier semaphores. Data moves between devices by JAX's collectives and lax.ppermute only.
A program may use at most 128 MiB of HBM per device.

```python
import math
import jax
import jax.numpy as jnp
from jax import lax

TOPICS = 512
VOCAB_DEV = 4096
WORD_BLOCK = 128
TILE_COUNT = 2
DOC_DEV = 16
ITERS = 2
SWEEPS = 4
DOCS = 512
VOCAB = 131072
WORD_BLOCKS = 32
N_DOC = 8
N_VOCAB = 4


def draw_seeds(key, part):
    key = jax.random.fold_in(key, 7)
    middle = jax.random.permutation(key, DOCS - 2)[:TOPICS - 2].astype(jnp.int32) + 1
    chosen = jnp.concatenate([jnp.array([0, DOCS - 1], jnp.int32), middle])
    return jax.random.permutation(jax.random.fold_in(key, 1), chosen).astype(jnp.int32)


def draw_count_tiles(key, part):
    key = jax.random.fold_in(key, 11)
    shards = VOCAB // VOCAB_DEV
    slots = TILE_COUNT * WORD_BLOCK * shards
    shape = (shards, shards, TILE_COUNT, DOC_DEV, WORD_BLOCK)
    background = max(1, 500 * 65536 // (2 * slots))
    dense_pick = jax.random.randint(jax.random.fold_in(key, 1), shape[:4] + (1,), 0, TILE_COUNT * shards)
    dense_tile = dense_pick < 8
    threshold = jnp.where(dense_tile, 9830, background)
    roll = jax.random.randint(jax.random.fold_in(key, 2), shape, 0, 65536)
    values = jax.random.randint(jax.random.fold_in(key, 3), shape, 1, 4)
    return jnp.where(roll < threshold, values, 0).astype(jnp.int32)


def draw_whitening(key, part):
    key = jax.random.fold_in(key, 13)
    noise_scale = 3000.0 ** (-0.5)
    row_blocks = VOCAB // WORD_BLOCK
    block_topic = jax.random.randint(jax.random.fold_in(key, 1), (row_blocks, 1, 1), 0, TOPICS)
    topic_ids = jnp.arange(TOPICS, dtype=jnp.int32)[None, None, :]
    noise = jnp.clip(jax.random.normal(jax.random.fold_in(key, 2), (row_blocks, WORD_BLOCK, TOPICS), jnp.float32), -4.0, 4.0) * noise_scale
    height = jnp.full((row_blocks, 1, 1), 0.05, jnp.float32)
    spike = jnp.where(block_topic == topic_ids, height, 0.0)
    return (noise + spike).reshape(VOCAB, TOPICS).astype(jnp.bfloat16)


def place_ends(drawn, rng, smallest, high):
    longest = drawn.shape.index(max(drawn.shape))
    spots = []
    for shift in (0, 1):
        where = [jax.random.randint(jax.random.fold_in(rng, axis), (), 0, length) for axis, length in enumerate(drawn.shape)]
        where[longest] = (where[longest] + shift) % drawn.shape[longest]
        spots.append(tuple(where))
    return drawn.at[spots[0]].set(smallest).at[spots[1]].set(high)


def setup_inputs(seed: int = 0) -> dict:
    splits = jax.random.split(jax.random.key(seed), 5)
    count_tiles = draw_count_tiles(jax.random.fold_in(splits[4], 71), 0)
    tile_words = place_ends(jax.random.randint(splits[1], (N_DOC * N_VOCAB, N_DOC * N_VOCAB, TILE_COUNT), 0, WORD_BLOCKS), jax.random.fold_in(splits[1], 1), 0, WORD_BLOCKS - 1).astype(jnp.int32)
    whitening = draw_whitening(jax.random.fold_in(splits[4], 71), 0)
    seeds = draw_seeds(jax.random.fold_in(splits[4], 71), 0)
    return {"count_tiles": count_tiles, "tile_words": tile_words, "whitening": whitening, "seeds": seeds}


SHIFT = 2.0
EPS = 1e-06
HIGHEST = lax.Precision.HIGHEST

def orthonormal(moment, current):
    shift_scale = TOPICS * jnp.sqrt(jnp.mean(moment * moment) + EPS)
    iterate = (moment + SHIFT * shift_scale * current) / ((SHIFT + 1.0) * shift_scale)
    for sweep_number in range(SWEEPS):
        gram_matrix = jnp.dot(iterate.T, iterate, precision=HIGHEST, preferred_element_type=jnp.float32)
        iterate = 1.5 * iterate - 0.5 * jnp.dot(iterate, gram_matrix, precision=HIGHEST, preferred_element_type=jnp.float32)
    return iterate

def whiten(count_tiles, tile_words, whitening):
    shard_count = N_DOC * N_VOCAB
    weight_shards = whitening.reshape(shard_count, VOCAB_DEV // WORD_BLOCK, WORD_BLOCK, TOPICS)

    def add_shard(running, pieces):
        tiles_one, words_one, table_one = pieces
        picked = jnp.take(table_one.astype(jnp.float32), words_one, axis=0)
        shard_term = jnp.einsum('btdw,btwk->bdk', tiles_one.astype(jnp.float32), picked, precision=HIGHEST)
        return (running + shard_term.reshape(DOCS, TOPICS), None)
    running, unused = lax.scan(add_shard, jnp.zeros((DOCS, TOPICS), jnp.float32), (count_tiles, tile_words, weight_shards))
    return running

def reference(count_tiles, tile_words, whitening, seeds):
    whitened = whiten(count_tiles, tile_words, whitening)
    current = orthonormal(whitened[seeds].T, jnp.eye(TOPICS, dtype=jnp.float32))
    for step_number in range(ITERS):
        projected = jnp.dot(whitened, current, precision=HIGHEST, preferred_element_type=jnp.float32)
        moment = jnp.dot(whitened.T, projected * projected, precision=HIGHEST, preferred_element_type=jnp.float32)
        current = orthonormal(moment, current)
    projected = jnp.dot(whitened, current, precision=HIGHEST, preferred_element_type=jnp.float32)
    weights = lax.optimization_barrier(jnp.sum(projected * projected * projected, axis=0)) / DOCS
    return (current * math.sqrt(TOPICS), weights)
```

```python
import functools
import math

import jax
import jax.numpy as jnp
from jax import lax
from jax.experimental import pallas as pl
from jax.experimental.pallas import tpu as pltpu
from jax.sharding import PartitionSpec as P

ITERS = 2
SWEEPS = 4
SHIFT = 2.0
EPS = 1e-06
AXES = ("doc", "vocab")
F32 = jnp.float32
BF16 = jnp.bfloat16
NN = (((1,), (0,)), ((), ()))
NT = (((1,), (1,)), ((), ()))


def split(value):
    high = value.astype(BF16)
    return high, (value - high.astype(F32)).astype(BF16)


def product(left, right, dims):
    left_high, left_low = split(left)
    right_high, right_low = split(right)
    dot = functools.partial(lax.dot_general, dimension_numbers=dims, preferred_element_type=F32)
    return dot(left_high, right_high) + (dot(left_high, right_low) + dot(left_low, right_high))


def plan(n_doc, n_vocab):
    n = n_doc * n_vocab
    bits = [1 << b for b in range(n.bit_length() - 1)]
    halving, whole = bits[:-2], bits[-2:]
    pairs = [(b, b) for b in halving]
    if len(halving) >= 3:
        pairs[1], pairs[2] = (halving[2], halving[1]), (halving[1], halving[2])
    return pairs, [(b, b) for b in whole]


def unit_at(place, me, pairs):
    steps = len(pairs)
    top = (place >> (steps - 1)) & 1
    odd = (me & 1) ^ top
    unit = (me & ((1 << steps) - 1)) ^ top
    for s in range(1, steps):
        even_mask, odd_mask = pairs[s]
        mask = even_mask + odd * (odd_mask - even_mask)
        unit = unit ^ (((place >> (steps - 1 - s)) & 1) * mask)
    return unit


def exchange(value, masks, n):
    perm = [(i, i ^ masks[i & 1]) for i in range(n)]
    return lax.ppermute(value, AXES, perm)


def whiten_kernel(pairs, unit_blocks, half_blocks, step_blocks, me_ref, words, tiles, table, keep, send, dense):
    step = pl.program_id(0)
    me = me_ref[0]
    doc_dev, word_block = tiles.shape[2], tiles.shape[3]
    dense[...] = jnp.zeros_like(dense)
    for local in range(2 * step_blocks):
        inside = local % step_blocks
        block_place = step * step_blocks + inside + (half_blocks if local >= step_blocks else 0)
        unit = unit_at(block_place // unit_blocks, me, pairs)
        block = unit * unit_blocks + block_place % unit_blocks
        rows = pl.ds(local * doc_dev, doc_dev)
        for t in range(tiles.shape[1]):
            columns = pl.ds(pl.multiple_of(words[block, t] * word_block, word_block), word_block)
            dense[rows, columns] = dense[rows, columns] + tiles[block, t].astype(F32).astype(BF16)
    rows = step_blocks * doc_dev
    send[...] = jnp.dot(dense[rows:, :], table[...], preferred_element_type=F32)
    keep[...] = jnp.dot(dense[:rows, :], table[...], preferred_element_type=F32)


def partial_rows(tiles, words, table, me, pairs):
    blocks, _, doc_dev, _ = tiles.shape
    topics = table.shape[1]
    unit_blocks = blocks >> len(pairs)
    half_blocks = blocks // 2
    step_blocks = math.gcd(half_blocks, 16)
    step_rows = step_blocks * doc_dev
    half = jax.ShapeDtypeStruct((half_blocks * doc_dev, topics), F32)
    out = pl.BlockSpec((step_rows, topics), lambda i: (i, 0))
    return pl.pallas_call(
        functools.partial(whiten_kernel, pairs, unit_blocks, half_blocks, step_blocks),
        grid=(half_blocks // step_blocks,),
        in_specs=[
            pl.BlockSpec(memory_space=pltpu.SMEM),
            pl.BlockSpec(memory_space=pltpu.SMEM),
            pl.BlockSpec(memory_space=pltpu.VMEM),
            pl.BlockSpec(memory_space=pltpu.VMEM),
        ],
        out_specs=[out, out],
        out_shape=[half, half],
        scratch_shapes=[pltpu.VMEM((2 * step_rows, table.shape[0]), BF16)],
        compiler_params=pltpu.CompilerParams(vmem_limit_bytes=40 << 20),
        name="whiten",
    )(me, words, tiles, table)


def iterate_kernel(chunk, docs_ref, seeds_ref, white_ref, basis_ref, weights_ref, moment_ref):
    topics = basis_ref.shape[0]
    docs = white_ref.shape[0]
    chunks = docs // chunk

    def rows_of(i):
        return pl.ds(pl.multiple_of(i * chunk, chunk), chunk)

    def projected(i):
        return product(basis_ref[...], white_ref[rows_of(i), :], NT)

    row = lax.broadcasted_iota(jnp.int32, (topics, topics), 0)
    column = lax.broadcasted_iota(jnp.int32, (topics, topics), 1)
    basis_ref[...] = jnp.where(row == column, 1.0, 0.0).astype(F32)

    def turn(number, carry):
        moment_ref[...] = jnp.zeros_like(moment_ref)

        def add(i, carry):
            @pl.when(number == 0)
            def _():
                hits = (seeds_ref[...] == docs_ref[i]).astype(F32).astype(BF16)
                high, low = split(white_ref[rows_of(i), :])
                moment_ref[...] += jnp.dot(hits, high, preferred_element_type=F32) + jnp.dot(
                    hits, low, preferred_element_type=F32
                )

            @pl.when(number > 0)
            def _():
                value = projected(i)
                moment_ref[...] += product(value * value, white_ref[rows_of(i), :], NN)

            return carry

        lax.fori_loop(0, chunks, add, 0)
        moment = moment_ref[...]
        scale = topics * jnp.sqrt(jnp.mean(moment * moment) + EPS)
        basis_ref[...] = (moment + SHIFT * scale * basis_ref[...]) / ((SHIFT + 1.0) * scale)

        def sweep(_, carry):
            current = basis_ref[...]
            gram = product(current, current, NT)
            basis_ref[...] = 1.5 * current - 0.5 * product(gram, current, NN)
            return carry

        lax.fori_loop(0, SWEEPS, sweep, 0)
        return carry

    lax.fori_loop(0, ITERS + 1, turn, 0)
    weights_ref[...] = jnp.zeros_like(weights_ref)

    def cubes(i, carry):
        value = projected(i)
        weights_ref[...] += jnp.sum(value * value * value, axis=1, keepdims=True)
        return carry

    lax.fori_loop(0, chunks, cubes, 0)
    weights_ref[...] = weights_ref[...] / docs


def iterate(white, docs_row, seeds):
    docs, topics = white.shape
    chunk = math.gcd(docs, 512)
    vmem = pl.BlockSpec(memory_space=pltpu.VMEM)
    return pl.pallas_call(
        functools.partial(iterate_kernel, chunk),
        in_specs=[vmem] * 3,
        out_specs=[vmem] * 2,
        out_shape=[
            jax.ShapeDtypeStruct((topics, topics), F32),
            jax.ShapeDtypeStruct((topics, 1), F32),
        ],
        scratch_shapes=[pltpu.VMEM((topics, topics), F32)],
        compiler_params=pltpu.CompilerParams(vmem_limit_bytes=40 << 20),
        name="iterate",
    )(docs_row.reshape(docs // chunk, 1, chunk), seeds.reshape(topics, 1), white)


def per_device(n_doc, n_vocab, count_tiles, tile_words, whitening, seeds):
    n = n_doc * n_vocab
    pairs, whole = plan(n_doc, n_vocab)
    me = lax.axis_index(AXES).astype(jnp.int32)
    keep, send = partial_rows(count_tiles[0], tile_words[0], whitening, me.reshape(1), pairs)
    docs, topics = keep.shape[0] * 2, keep.shape[1]
    unit_rows = docs >> len(pairs)
    value = keep + exchange(send, pairs[0], n)
    for masks in pairs[1:]:
        half = value.shape[0] // 2
        value = value[:half] + exchange(value[half:], masks, n)
    for masks in whole:
        value = value + exchange(value, masks, n)
    for masks in reversed(pairs):
        value = jnp.concatenate([value, exchange(value, masks, n)])
    place = jnp.arange(docs, dtype=jnp.int32)
    docs_row = unit_at(place // unit_rows, me, pairs) * unit_rows + place % unit_rows
    basis, weights = iterate(value, docs_row, seeds)
    own_rows = topics // n_vocab
    own = lax.dynamic_slice_in_dim(basis, lax.axis_index("vocab") * own_rows, own_rows, 1)
    return own.T * math.sqrt(topics), weights.reshape(topics)


def solution(mesh):
    in_specs = (
        P(("doc", "vocab"), None, None, None, None),
        P(("doc", "vocab"), None, None),
        P(("doc", "vocab"), None),
        P(),
    )
    out_specs = (P("vocab", None), P())
    return jax.shard_map(
        functools.partial(per_device, mesh.shape["doc"], mesh.shape["vocab"]),
        mesh=mesh,
        in_specs=in_specs,
        out_specs=out_specs,
        check_vma=False,
    )
```

```python
import functools
import math

import jax
import jax.numpy as jnp
from jax import lax
from jax.experimental import pallas as pl
from jax.experimental.pallas import tpu as pltpu
from jax.sharding import PartitionSpec as P

ITERS = 2
SWEEPS = 4
SHIFT = 2.0
EPS = 1e-06
AXES = ("doc", "vocab")
F32 = jnp.float32
BF16 = jnp.bfloat16
NN = (((1,), (0,)), ((), ()))
NT = (((1,), (1,)), ((), ()))


def split(value):
    high = value.astype(BF16)
    return high, (value - high.astype(F32)).astype(BF16)


def dot(left, right, dims):
    return lax.dot_general(left, right, dims, preferred_element_type=F32)


def product(left, right, dims):
    high = dot(left[0], right[0], dims)
    return high + (dot(left[0], right[1], dims) + dot(left[1], right[0], dims))


def plan(n_doc, n_vocab):
    n = n_doc * n_vocab
    bits = [1 << b for b in range(n.bit_length() - 1)]
    halving, whole = bits[:-2], bits[-2:]
    pairs = [(b, b) for b in halving]
    if len(halving) >= 3:
        pairs[1], pairs[2] = (halving[2], halving[1]), (halving[1], halving[2])
    return pairs, [(b, b) for b in whole]


def unit_at(place, me, pairs):
    steps = len(pairs)
    top = (place >> (steps - 1)) & 1
    odd = (me & 1) ^ top
    unit = (me & ((1 << steps) - 1)) ^ top
    for s in range(1, steps):
        even_mask, odd_mask = pairs[s]
        mask = even_mask + odd * (odd_mask - even_mask)
        unit = unit ^ (((place >> (steps - 1 - s)) & 1) * mask)
    return unit


def exchange(value, masks, n):
    perm = [(i, i ^ masks[i & 1]) for i in range(n)]
    return lax.ppermute(value, AXES, perm)


def whiten_kernel(pairs, unit_blocks, half_blocks, step_blocks, chains, me_ref, words, tiles_in, table, *rest):
    outs, (dense, tiles, held, tile_sem, sems) = rest[: 2 * chains], rest[2 * chains :]
    steps = half_blocks // step_blocks
    step = pl.program_id(0) if steps > 1 else 0
    me = me_ref[0]
    doc_dev, word_block = tiles.shape[2], tiles.shape[3]
    chain_blocks = unit_blocks // chains
    chunk = held.shape[0] // CHUNKS
    cuts = [slice(k * chunk, (k + 1) * chunk) for k in range(CHUNKS)]
    fetch_tiles = pltpu.make_async_copy(tiles_in, tiles, tile_sem)
    fetches = [pltpu.make_async_copy(table.at[cut], held.at[cut], sems.at[k]) for k, cut in enumerate(cuts)]

    def first(action):
        if steps > 1:
            pl.when(step == 0)(action)
        else:
            action()

    @first
    def _():
        fetch_tiles.start()
        for fetch in fetches[:AHEAD]:
            fetch.start()

    dense[...] = jnp.zeros_like(dense)
    first(fetch_tiles.wait)
    for part in range(2 * chains):
        for inside in range(step_blocks):
            place = step * step_blocks + inside + (part % 2) * half_blocks
            unit = unit_at(place // chain_blocks, me, pairs)
            block = unit * unit_blocks + (part // 2) * chain_blocks + place % chain_blocks
            rows = pl.ds((part * step_blocks + inside) * doc_dev, doc_dev)
            for t in range(tiles.shape[1]):
                columns = pl.ds(pl.multiple_of(words[t, block] * word_block, word_block), word_block)
                dense[rows, columns] = dense[rows, columns] + tiles[block, t].astype(F32).astype(BF16)

    value = None
    for k, cut in enumerate(cuts):
        first(fetches[k].wait)
        if k + AHEAD < CHUNKS:
            first(fetches[k + AHEAD].start)
        term = dot(dense[:, cut], held[cut, :], NN)
        value = term if value is None else value + term
    rows = step_blocks * doc_dev
    for part in range(2 * chains):
        outs[part][...] = value[part * rows : (part + 1) * rows]


def partial_rows(tiles, words, table, me, pairs, chains):
    blocks, _, doc_dev, _ = tiles.shape
    topics = table.shape[1]
    unit_blocks = blocks >> len(pairs)
    half_blocks = blocks // 2 // chains
    step_blocks = math.gcd(half_blocks, 16 // chains)
    steps = half_blocks // step_blocks
    step_rows = step_blocks * doc_dev
    half = jax.ShapeDtypeStruct((half_blocks * doc_dev, topics), F32)
    if steps > 1:
        out = pl.BlockSpec((step_rows, topics), lambda i: (i, 0))
    else:
        out = pl.BlockSpec(memory_space=pltpu.VMEM)
    return pl.pallas_call(
        functools.partial(whiten_kernel, pairs, unit_blocks, half_blocks, step_blocks, chains),
        grid=(steps,) if steps > 1 else (),
        in_specs=[
            pl.BlockSpec(memory_space=pltpu.SMEM),
            pl.BlockSpec(memory_space=pltpu.SMEM),
            pl.BlockSpec(memory_space=pl.ANY),
            pl.BlockSpec(memory_space=pl.ANY),
        ],
        out_specs=[out] * (2 * chains),
        out_shape=[half] * (2 * chains),
        scratch_shapes=[
            pltpu.VMEM((2 * chains * step_rows, table.shape[0]), BF16),
            pltpu.VMEM(tiles.shape, jnp.int32),
            pltpu.VMEM(table.shape, BF16),
            pltpu.SemaphoreType.DMA,
            pltpu.SemaphoreType.DMA((CHUNKS,)),
        ],
        compiler_params=pltpu.CompilerParams(vmem_limit_bytes=VMEM_LIMIT),
        name="whiten",
    )(me, words, tiles, table)


def orthonormal(basis_ref, diff_ref, factor_ref):
    topics = basis_ref.shape[0]
    start = (SHIFT / (SHIFT + 1.0)) ** 2
    basis = split(basis_ref[...])
    row = lax.broadcasted_iota(jnp.int32, (topics, topics), 0)
    column = lax.broadcasted_iota(jnp.int32, (topics, topics), 1)
    diff = jnp.where(row == column, start, 0.0).astype(F32) - product(basis, basis, NT)
    e = 1.0 - start
    q = 1.0 + e / 2
    factor = 0.5 * diff
    for sweep in range(1, SWEEPS):
        low = diff.astype(BF16)
        square = dot(low, low, NN)
        mixed = ((3 + 3 * e) / 4) * diff + 0.25 * square
        diff = ((6 * e + 3 * e * e) / 4) * diff + dot(low, mixed.astype(BF16), NN)
        e = (3 * e * e + e * e * e) / 4
        factor = (1.0 + e / 2) * factor + (0.5 * q) * diff + 0.5 * dot(
            factor.astype(BF16), diff.astype(BF16), NN
        )
        q = q * (1.0 + e / 2)
    basis_ref[...] = q * basis_ref[...] + product(split(factor), basis, NN)


def iterate_kernel(chunk, own_ref, docs_ref, seeds_ref, *rest):
    pieces, (own_out, weights_ref, basis_ref, moment_ref, high_ref, low_ref) = rest[:-6], rest[-6:]
    topics = basis_ref.shape[0]
    docs = high_ref.shape[0]
    chunks = docs // chunk
    first = 0
    for piece in pieces:
        rows = slice(first, first + piece.shape[0])
        first = first + piece.shape[0]
        high, low = split(piece[...])
        high_ref[rows, :] = high
        low_ref[rows, :] = low

    def white(i):
        rows = pl.ds(pl.multiple_of(i * chunk, chunk), chunk)
        return high_ref[rows, :], low_ref[rows, :]

    row = lax.broadcasted_iota(jnp.int32, (topics, topics), 0)
    column = lax.broadcasted_iota(jnp.int32, (topics, topics), 1)
    basis_ref[...] = jnp.where(row == column, 1.0, 0.0).astype(F32)

    def turn(number, carry):
        moment_ref[...] = jnp.zeros_like(moment_ref)

        def add(i, carry):
            high, low = white(i)

            @pl.when(number == 0)
            def _():
                hits = (seeds_ref[...] == docs_ref[i]).astype(F32).astype(BF16)
                moment_ref[...] += dot(hits, high, NN) + dot(hits, low, NN)

            @pl.when(number > 0)
            def _():
                value = product(split(basis_ref[...]), (high, low), NT)
                moment_ref[...] += product(split(value * value), (high, low), NN)

            return carry

        lax.fori_loop(0, chunks, add, 0)
        moment = moment_ref[...]
        scale = topics * jnp.sqrt(jnp.mean(moment * moment) + EPS)
        basis_ref[...] = moment * (1.0 / ((SHIFT + 1.0) * scale)) + (SHIFT / (SHIFT + 1.0)) * basis_ref[...]
        orthonormal(basis_ref, None, None)
        return carry

    lax.fori_loop(0, ITERS + 1, turn, 0)
    parts = split(basis_ref[...])
    total = jnp.zeros((1, topics), F32)
    for i in range(chunks):
        value = product(white(i), parts, NT)
        total += jnp.sum(value * value * value, axis=0, keepdims=True)
    weights_ref[...] = total / docs
    moment_ref[...] = basis_ref[...].T * math.sqrt(topics)
    own_rows = own_out.shape[0]
    own_out[...] = moment_ref[pl.ds(pl.multiple_of(own_ref[0] * own_rows, own_rows), own_rows), :]


def iterate(pieces, docs_row, seeds, own, own_rows):
    docs = docs_row.shape[0]
    topics = seeds.shape[0]
    chunk = math.gcd(docs, 512)
    vmem = pl.BlockSpec(memory_space=pltpu.VMEM)
    return pl.pallas_call(
        functools.partial(iterate_kernel, chunk),
        in_specs=[pl.BlockSpec(memory_space=pltpu.SMEM)] + [vmem] * (2 + len(pieces)),
        out_specs=[vmem] * 2,
        out_shape=[
            jax.ShapeDtypeStruct((own_rows, topics), F32),
            jax.ShapeDtypeStruct((1, topics), F32),
        ],
        scratch_shapes=[
            pltpu.VMEM((topics, topics), F32),
            pltpu.VMEM((topics, topics), F32),
            pltpu.VMEM((docs, topics), BF16),
            pltpu.VMEM((docs, topics), BF16),
        ],
        compiler_params=pltpu.CompilerParams(vmem_limit_bytes=40 << 20),
        name="iterate",
    )(own, docs_row.reshape(docs // chunk, 1, chunk), seeds.reshape(topics, 1), *pieces)


CHAINS = 2
VMEM_LIMIT = 53 << 20
CHUNKS = 4
AHEAD = 2
SWAP = True


def per_device(n_doc, n_vocab, count_tiles, tile_words, whitening, seeds):
    n = n_doc * n_vocab
    pairs, whole = plan(n_doc, n_vocab)
    me = lax.axis_index(AXES).astype(jnp.int32)
    halves = partial_rows(count_tiles[0], tile_words[0].T, whitening, me.reshape(1), pairs, CHAINS)
    rows, topics = halves[0].shape[0] * 2, whitening.shape[1]
    docs = rows * CHAINS
    values = [keep + exchange(send, pairs[0], n) for keep, send in zip(halves[::2], halves[1::2])]
    half = rows // 2
    for masks in pairs[1:]:
        half = half // 2
        values = [v[:half] + exchange(v[half:], masks, n) for v in values]
    for s in range(len(whole)):
        values = [v + exchange(v, whole[s ^ (c & 1) if SWAP else s], n) for c, v in enumerate(values)]
    for masks in reversed(pairs[1:]):
        values = [jnp.concatenate([v, exchange(v, masks, n)]) for v in values]
    pieces = []
    for v in values:
        pieces += [v, exchange(v, pairs[0], n)]
    place = jnp.arange(docs, dtype=jnp.int32)
    chain_rows = (docs >> len(pairs)) // CHAINS
    unit = unit_at(place % rows // chain_rows, me, pairs)
    docs_row = unit * (chain_rows * CHAINS) + place // rows * chain_rows + place % chain_rows
    own = lax.axis_index("vocab").astype(jnp.int32).reshape(1)
    directions, weights = iterate(pieces, docs_row, seeds, own, topics // n_vocab)
    return directions, weights.reshape(topics)


def solution(mesh):
    in_specs = (
        P(("doc", "vocab"), None, None, None, None),
        P(("doc", "vocab"), None, None),
        P(("doc", "vocab"), None),
        P(),
    )
    out_specs = (P("vocab", None), P())
    return jax.shard_map(
        functools.partial(per_device, mesh.shape["doc"], mesh.shape["vocab"]),
        mesh=mesh,
        in_specs=in_specs,
        out_specs=out_specs,
        check_vma=False,
    )
```

```python
import functools
import math

import jax
import jax.numpy as jnp
from jax import lax
from jax.experimental import pallas as pl
from jax.experimental.pallas import tpu as pltpu
from jax.sharding import PartitionSpec as P

ITERS = 2
SWEEPS = 4
SHIFT = 2.0
EPS = 1e-06
AXES = ("doc", "vocab")
F32 = jnp.float32
BF16 = jnp.bfloat16
NN = (((1,), (0,)), ((), ()))
NT = (((1,), (1,)), ((), ()))


def split(value):
    high = value.astype(BF16)
    return high, (value - high.astype(F32)).astype(BF16)


def dot(left, right, dims):
    return lax.dot_general(left, right, dims, preferred_element_type=F32)


def product(left, right, dims):
    high = dot(left[0], right[0], dims)
    return high + (dot(left[0], right[1], dims) + dot(left[1], right[0], dims))


def plan(n_doc, n_vocab):
    n = n_doc * n_vocab
    bits = [1 << b for b in range(n.bit_length() - 1)]
    halving, whole = bits[:-2], bits[-2:]
    pairs = [(b, b) for b in halving]
    if len(halving) >= 3:
        pairs[1], pairs[2] = (halving[2], halving[1]), (halving[1], halving[2])
    return pairs, [(b, b) for b in whole]


def unit_at(place, me, pairs):
    steps = len(pairs)
    top = (place >> (steps - 1)) & 1
    odd = (me & 1) ^ top
    unit = (me & ((1 << steps) - 1)) ^ top
    for s in range(1, steps):
        even_mask, odd_mask = pairs[s]
        mask = even_mask + odd * (odd_mask - even_mask)
        unit = unit ^ (((place >> (steps - 1 - s)) & 1) * mask)
    return unit


def position():
    return lax.axis_index("doc") * lax.axis_size("vocab") + lax.axis_index("vocab")


def exchange(value, masks, n):
    perm = [(i, i ^ masks[i & 1]) for i in range(n)]
    return lax.ppermute(value, AXES, perm)


def whiten_kernel(pairs, unit_blocks, half_blocks, step_blocks, chains, words_in, tiles_in, table, *rest):
    outs, (words, dense, tiles, held, word_sem, tile_sem, sems) = rest[: 2 * chains], rest[2 * chains :]
    steps = half_blocks // step_blocks
    step = pl.program_id(0) if steps > 1 else 0
    me = position()
    doc_dev, word_block = tiles.shape[2], tiles.shape[3]
    chain_blocks = unit_blocks // chains
    chunk = held.shape[0] // CHUNKS
    cuts = [slice(k * chunk, (k + 1) * chunk) for k in range(CHUNKS)]
    fetch_words = pltpu.make_async_copy(words_in, words, word_sem)
    fetch_tiles = pltpu.make_async_copy(tiles_in, tiles, tile_sem)
    fetches = [pltpu.make_async_copy(table.at[cut], held.at[cut], sems.at[k]) for k, cut in enumerate(cuts)]

    def first(action):
        if steps > 1:
            pl.when(step == 0)(action)
        else:
            action()

    @first
    def _():
        fetch_words.start()
        fetch_tiles.start()
        for fetch in fetches[:AHEAD]:
            fetch.start()

    dense[...] = jnp.zeros_like(dense)
    first(fetch_words.wait)
    first(fetch_tiles.wait)
    for part in range(2 * chains):
        for inside in range(step_blocks):
            place = step * step_blocks + inside + (part % 2) * half_blocks
            unit = unit_at(place // chain_blocks, me, pairs)
            block = unit * unit_blocks + (part // 2) * chain_blocks + place % chain_blocks
            rows = pl.ds((part * step_blocks + inside) * doc_dev, doc_dev)
            for t in range(tiles.shape[1]):
                columns = pl.ds(pl.multiple_of(words[t, block] * word_block, word_block), word_block)
                dense[rows, columns] = dense[rows, columns] + tiles[block, t].astype(F32).astype(BF16)

    value = None
    for k, cut in enumerate(cuts):
        first(fetches[k].wait)
        if k + AHEAD < CHUNKS:
            first(fetches[k + AHEAD].start)
        term = dot(dense[:, cut], held[cut, :], NN)
        value = term if value is None else value + term
    rows = step_blocks * doc_dev
    for part in range(2 * chains):
        outs[part][...] = value[part * rows : (part + 1) * rows]


def partial_rows(tiles, words, table, pairs, chains):
    blocks, _, doc_dev, _ = tiles.shape
    topics = table.shape[1]
    unit_blocks = blocks >> len(pairs)
    half_blocks = blocks // 2 // chains
    step_blocks = math.gcd(half_blocks, 16 // chains)
    steps = half_blocks // step_blocks
    step_rows = step_blocks * doc_dev
    half = jax.ShapeDtypeStruct((half_blocks * doc_dev, topics), F32)
    if steps > 1:
        out = pl.BlockSpec((step_rows, topics), lambda i: (i, 0))
    else:
        out = pl.BlockSpec(memory_space=pltpu.VMEM)
    return pl.pallas_call(
        functools.partial(whiten_kernel, pairs, unit_blocks, half_blocks, step_blocks, chains),
        grid=(steps,) if steps > 1 else (),
        in_specs=[
            pl.BlockSpec(memory_space=pl.ANY),
            pl.BlockSpec(memory_space=pl.ANY),
            pl.BlockSpec(memory_space=pl.ANY),
        ],
        out_specs=[out] * (2 * chains),
        out_shape=[half] * (2 * chains),
        scratch_shapes=[
            pltpu.SMEM(words.shape, jnp.int32),
            pltpu.VMEM((2 * chains * step_rows, table.shape[0]), BF16),
            pltpu.VMEM(tiles.shape, jnp.int32),
            pltpu.VMEM(table.shape, BF16),
            pltpu.SemaphoreType.DMA,
            pltpu.SemaphoreType.DMA,
            pltpu.SemaphoreType.DMA((CHUNKS,)),
        ],
        compiler_params=pltpu.CompilerParams(vmem_limit_bytes=VMEM_LIMIT),
        name="whiten",
    )(words, tiles, table)


def series(e):
    return (
        1.0 + e / 2 + 0.375 * e**2 + 0.3125 * e**3 + 0.0625 * e**4,
        0.5 + 0.75 * e + 0.9375 * e**2 + 0.25 * e**3,
        0.375 + 0.9375 * e + 0.375 * e**2,
        0.3125 + 0.25 * e,
        0.0625,
    )


def following(e):
    return (3 * e**2 + e**3) / 4, (6 * e + 3 * e**2) / 4, (3 + 3 * e) / 4, 0.25


def iterate_kernel(chunk, pairs, chains, seeds_ref, *rest):
    refs, pieces = rest[-SCRATCH - 2 :], rest[: -SCRATCH - 2]
    own_out, weights_ref, basis, white_high, white_low, basis_high, basis_low, diff_high, factor_high, square_high = refs
    topics = basis.shape[0]
    docs = white_high.shape[0]
    chunks = docs // chunk
    blocks = [slice(r, r + BLOCK) for r in range(0, topics, BLOCK)]
    each = range(len(blocks))
    first = 0
    for piece in pieces:
        rows = slice(first, first + piece.shape[0])
        first = first + piece.shape[0]
        white_high[rows, :], white_low[rows, :] = split(piece[...])

    def diagonal(rows, value):
        row = lax.broadcasted_iota(jnp.int32, (BLOCK, topics), 0) + rows.start
        column = lax.broadcasted_iota(jnp.int32, (BLOCK, topics), 1)
        return jnp.where(row == column, value, 0.0).astype(F32)

    def over_chunks(term):
        if chunks == 1:
            return term(0, slice(0, docs))

        def add(i, totals):
            terms = term(i, pl.ds(pl.multiple_of(i * chunk, chunk), chunk))
            return [total + one for total, one in zip(totals, terms)]

        return lax.fori_loop(0, chunks, add, [jnp.zeros((BLOCK, topics), F32) for _ in blocks])

    me = position()
    chain = docs // chains
    unit_rows = docs >> len(pairs)
    part_rows = unit_rows // chains

    def docs_of(i):
        place = lax.broadcasted_iota(jnp.int32, (1, chunk), 1) + i * chunk
        inside = lax.rem(place, chain)
        unit = unit_at(lax.div(inside, part_rows), me, pairs)
        return unit * unit_rows + lax.div(place, chain) * part_rows + lax.rem(inside, part_rows)

    def picked(i, docs_rows):
        hits = [(seeds_ref[rows, :] == docs_of(i)).astype(F32).astype(BF16) for rows in blocks]
        white = white_high[docs_rows, :]
        return [dot(hit, white, NN) for hit in hits]

    def moments(i, docs_rows):
        high, low = white_high[docs_rows, :], white_low[docs_rows, :]
        value = [dot(basis_high[rows, :], high, NT) + dot(basis_high[rows, :], low, NT) for rows in blocks]
        value = [split(v * v) for v in value]
        return [product(v, (high, low), NN) for v in value]

    def orthonormal(term, current):
        moment = over_chunks(term)
        norm = sum(jnp.sum(v * v) for v in moment)
        scale = topics * jnp.sqrt(norm / (topics * topics) + EPS)
        start = SHIFT / (SHIFT + 1.0)
        weight = 1.0 / ((SHIFT + 1.0) * scale)
        for v, rows in zip(moment, blocks):
            value = v * weight + start * current(rows)
            basis[rows, :] = value
            basis_high[rows, :], basis_low[rows, :] = split(value)
        both = (basis_high[...], basis_low[...])
        gram = [product((basis_high[rows, :], basis_low[rows, :]), both, NT) for rows in blocks]
        diff = [diagonal(rows, start * start) - g for g, rows in zip(gram, blocks)]
        e = 1.0 - start * start
        q = 1.0
        for pair in range(SWEEPS // 2):
            for step in range(2):
                for d, rows in zip(diff, blocks):
                    diff_high[rows, :] = d.astype(BF16)
                whole = diff_high[...]
                second = [dot(diff_high[rows, :], whole, NN) for rows in blocks]
                if pair < SWEEPS // 2 - 1:
                    third = [dot(v.astype(BF16), whole, NN) for v in second]
                if step == 0:
                    c0, c1, c2, c3, c4 = series(e)
                    value = [c1 * diff[k] + c2 * second[k] for k in each]
                    for v, rows in zip(second, blocks):
                        square_high[rows, :] = v.astype(BF16)
                    square = square_high[...]
                    mixed = [(c3 * diff[k] + c4 * second[k]).astype(BF16) for k in each]
                    value = [value[k] + dot(mixed[k], square, NN) for k in each]
                    if pair == 0:
                        factor = value
                        for f, rows in zip(factor, blocks):
                            factor_high[rows, :] = f.astype(BF16)
                    else:
                        before = factor_high[...]
                        factor = [
                            q * value[k] + c0 * factor[k] + dot(value[k].astype(BF16), before, NN) for k in each
                        ]
                    q = q * c0
                if pair == SWEEPS // 2 - 1:
                    break
                e, c1, c2, c3 = following(e)
                diff = [c1 * diff[k] + c2 * second[k] + c3 * third[k] for k in each]
        parts = [split(f) for f in factor]
        value = [q * basis[rows, :] + product(parts[k], both, NN) for k, rows in enumerate(blocks)]
        for v, rows in zip(value, blocks):
            basis[rows, :] = v
            basis_high[rows, :], basis_low[rows, :] = split(v)

    orthonormal(picked, lambda rows: diagonal(rows, 1.0))

    def turn(_, carry):
        orthonormal(moments, lambda rows: basis[rows, :])
        return carry

    lax.fori_loop(0, ITERS, turn, 0)
    parts = (basis_high[...], basis_low[...])
    total = jnp.zeros((1, topics), F32)
    for r in range(0, docs, chunk):
        value = product((white_high[r : r + chunk, :], white_low[r : r + chunk, :]), parts, NT)
        total += jnp.sum(value * value * value, axis=0, keepdims=True)
    weights_ref[...] = total / docs
    basis[...] = basis[...].T * math.sqrt(topics)
    own_rows = own_out.shape[0]
    own_out[...] = basis[pl.ds(pl.multiple_of(lax.axis_index("vocab") * own_rows, own_rows), own_rows), :]


def iterate(pieces, seeds, docs, pairs, own_rows):
    topics = seeds.shape[0]
    chunk = math.gcd(docs, 512)
    vmem = pl.BlockSpec(memory_space=pltpu.VMEM)
    return pl.pallas_call(
        functools.partial(iterate_kernel, chunk, pairs, CHAINS),
        in_specs=[vmem] * (1 + len(pieces)),
        out_specs=[vmem] * 2,
        out_shape=[
            jax.ShapeDtypeStruct((own_rows, topics), F32),
            jax.ShapeDtypeStruct((1, topics), F32),
        ],
        scratch_shapes=[
            pltpu.VMEM((topics, topics), F32),
            *[pltpu.VMEM((docs, topics), BF16)] * 2,
            *[pltpu.VMEM((topics, topics), BF16)] * 5,
        ],
        compiler_params=pltpu.CompilerParams(vmem_limit_bytes=40 << 20),
        name="iterate",
    )(seeds.reshape(topics, 1), *pieces)


CHAINS = 2
SCRATCH = 8
BLOCK = 256
VMEM_LIMIT = 53 << 20
CHUNKS = 4
AHEAD = 2
SWAP = True


def per_device(n_doc, n_vocab, count_tiles, tile_words, whitening, seeds):
    n = n_doc * n_vocab
    pairs, whole = plan(n_doc, n_vocab)
    halves = partial_rows(count_tiles[0], tile_words[0].T, whitening, pairs, CHAINS)
    rows, topics = halves[0].shape[0] * 2, whitening.shape[1]
    docs = rows * CHAINS
    values = [keep + exchange(send, pairs[0], n) for keep, send in zip(halves[::2], halves[1::2])]
    half = rows // 2
    for masks in pairs[1:]:
        half = half // 2
        values = [v[:half] + exchange(v[half:], masks, n) for v in values]
    for s in range(len(whole)):
        values = [v + exchange(v, whole[s ^ (c & 1) if SWAP else s], n) for c, v in enumerate(values)]
    for masks in reversed(pairs[1:]):
        values = [jnp.concatenate([v, exchange(v, masks, n)]) for v in values]
    pieces = []
    for v in values:
        pieces += [v, exchange(v, pairs[0], n)]
    directions, weights = iterate(pieces, seeds, docs, pairs, topics // n_vocab)
    return directions, weights.reshape(topics)


def solution(mesh):
    in_specs = (
        P(("doc", "vocab"), None, None, None, None),
        P(("doc", "vocab"), None, None),
        P(("doc", "vocab"), None),
        P(),
    )
    out_specs = (P("vocab", None), P())
    return jax.shard_map(
        functools.partial(per_device, mesh.shape["doc"], mesh.shape["vocab"]),
        mesh=mesh,
        in_specs=in_specs,
        out_specs=out_specs,
        check_vma=False,
    )
```

```python
import functools
import math

import jax
import jax.numpy as jnp
from jax import lax
from jax.experimental import pallas as pl
from jax.experimental.pallas import tpu as pltpu
from jax.sharding import PartitionSpec as P

ITERS = 2
SWEEPS = 4
SHIFT = 2.0
EPS = 1e-06
AXES = ("doc", "vocab")
F32 = jnp.float32
BF16 = jnp.bfloat16
NN = (((1,), (0,)), ((), ()))
NT = (((1,), (1,)), ((), ()))


def split(value):
    high = value.astype(BF16)
    return high, (value - high.astype(F32)).astype(BF16)


def dot(left, right, dims):
    return lax.dot_general(left, right, dims, preferred_element_type=F32)


def product(left, right, dims):
    high = dot(left[0], right[0], dims)
    return high + (dot(left[0], right[1], dims) + dot(left[1], right[0], dims))


def plan(n_doc, n_vocab):
    n = n_doc * n_vocab
    bits = [1 << b for b in range(n.bit_length() - 1)]
    halving, whole = bits[:-2], bits[-2:]
    pairs = [(b, b) for b in halving]
    if len(halving) >= 3:
        pairs[1], pairs[2] = (halving[2], halving[1]), (halving[1], halving[2])
    return pairs, [(b, b) for b in whole]


def unit_at(place, me, pairs):
    steps = len(pairs)
    top = (place >> (steps - 1)) & 1
    odd = (me & 1) ^ top
    unit = (me & ((1 << steps) - 1)) ^ top
    for s in range(1, steps):
        even_mask, odd_mask = pairs[s]
        mask = even_mask + odd * (odd_mask - even_mask)
        unit = unit ^ (((place >> (steps - 1 - s)) & 1) * mask)
    return unit


def position():
    return lax.axis_index("doc") * lax.axis_size("vocab") + lax.axis_index("vocab")


def exchange(value, masks, n):
    perm = [(i, i ^ masks[i & 1]) for i in range(n)]
    return lax.ppermute(value, AXES, perm)


def whiten_kernel(pairs, unit_blocks, half_blocks, step_blocks, chains, words_in, tiles_in, table, *rest):
    outs, (words, dense, tiles, held, word_sem, tile_sem, sems) = rest[: 2 * chains], rest[2 * chains :]
    steps = half_blocks // step_blocks
    step = pl.program_id(0) if steps > 1 else 0
    me = position()
    doc_dev, word_block = tiles.shape[2], tiles.shape[3]
    chain_blocks = unit_blocks // chains
    chunk = held.shape[0] // CHUNKS
    cuts = [slice(k * chunk, (k + 1) * chunk) for k in range(CHUNKS)]
    fetch_words = pltpu.make_async_copy(words_in, words, word_sem)
    fetch_tiles = pltpu.make_async_copy(tiles_in, tiles, tile_sem)
    fetches = [pltpu.make_async_copy(table.at[cut], held.at[cut], sems.at[k]) for k, cut in enumerate(cuts)]

    def first(action):
        if steps > 1:
            pl.when(step == 0)(action)
        else:
            action()

    @first
    def _():
        fetch_words.start()
        fetch_tiles.start()
        for fetch in fetches[:AHEAD]:
            fetch.start()

    dense[...] = jnp.zeros_like(dense)
    first(fetch_words.wait)
    first(fetch_tiles.wait)
    for part in range(2 * chains):
        for inside in range(step_blocks):
            place = step * step_blocks + inside + (part % 2) * half_blocks
            unit = unit_at(place // chain_blocks, me, pairs)
            block = unit * unit_blocks + (part // 2) * chain_blocks + place % chain_blocks
            rows = pl.ds((part * step_blocks + inside) * doc_dev, doc_dev)
            for t in range(tiles.shape[1]):
                columns = pl.ds(pl.multiple_of(words[t, block] * word_block, word_block), word_block)
                dense[rows, columns] = dense[rows, columns] + tiles[block, t].astype(F32).astype(BF16)

    value = None
    for k, cut in enumerate(cuts):
        first(fetches[k].wait)
        if k + AHEAD < CHUNKS:
            first(fetches[k + AHEAD].start)
        term = dot(dense[:, cut], held[cut, :], NN)
        value = term if value is None else value + term
    rows = step_blocks * doc_dev
    for part in range(2 * chains):
        outs[part][...] = value[part * rows : (part + 1) * rows]


def partial_rows(tiles, words, table, pairs, chains):
    blocks, _, doc_dev, _ = tiles.shape
    topics = table.shape[1]
    unit_blocks = blocks >> len(pairs)
    half_blocks = blocks // 2 // chains
    step_blocks = math.gcd(half_blocks, 16 // chains)
    steps = half_blocks // step_blocks
    step_rows = step_blocks * doc_dev
    half = jax.ShapeDtypeStruct((half_blocks * doc_dev, topics), F32)
    if steps > 1:
        out = pl.BlockSpec((step_rows, topics), lambda i: (i, 0))
    else:
        out = pl.BlockSpec(memory_space=pltpu.VMEM)
    return pl.pallas_call(
        functools.partial(whiten_kernel, pairs, unit_blocks, half_blocks, step_blocks, chains),
        grid=(steps,) if steps > 1 else (),
        in_specs=[
            pl.BlockSpec(memory_space=pl.ANY),
            pl.BlockSpec(memory_space=pl.ANY),
            pl.BlockSpec(memory_space=pl.ANY),
        ],
        out_specs=[out] * (2 * chains),
        out_shape=[half] * (2 * chains),
        scratch_shapes=[
            pltpu.SMEM(words.shape, jnp.int32),
            pltpu.VMEM((2 * chains * step_rows, table.shape[0]), BF16),
            pltpu.VMEM(tiles.shape, jnp.int32),
            pltpu.VMEM(table.shape, BF16),
            pltpu.SemaphoreType.DMA,
            pltpu.SemaphoreType.DMA,
            pltpu.SemaphoreType.DMA((CHUNKS,)),
        ],
        compiler_params=pltpu.CompilerParams(vmem_limit_bytes=VMEM_LIMIT),
        name="whiten",
    )(words, tiles, table)


def series(e):
    return (
        1.0 + e / 2 + 0.375 * e**2 + 0.3125 * e**3 + 0.0625 * e**4,
        0.5 + 0.75 * e + 0.9375 * e**2 + 0.25 * e**3,
        0.375 + 0.9375 * e + 0.375 * e**2,
        0.3125 + 0.25 * e,
        0.0625,
    )


def following(e):
    return (3 * e**2 + e**3) / 4, (6 * e + 3 * e**2) / 4, (3 + 3 * e) / 4, 0.25


def iterate_kernel(chunk, pairs, chains, seeds_ref, *rest):
    refs, pieces = rest[-SCRATCH - 2 :], rest[: -SCRATCH - 2]
    own_out, weights_ref, basis, white_high, white_low, basis_high, basis_low, diff_high, factor_high, square_high = refs
    topics = basis.shape[0]
    docs = white_high.shape[0]
    chunks = docs // chunk
    blocks = [slice(r, r + BLOCK) for r in range(0, topics, BLOCK)]
    each = range(len(blocks))
    first = 0
    for piece in pieces:
        rows = slice(first, first + piece.shape[0])
        first = first + piece.shape[0]
        white_high[rows, :], white_low[rows, :] = split(piece[...])

    def diagonal(rows, value):
        row = lax.broadcasted_iota(jnp.int32, (BLOCK, topics), 0) + rows.start
        column = lax.broadcasted_iota(jnp.int32, (BLOCK, topics), 1)
        return jnp.where(row == column, value, 0.0).astype(F32)

    def over_chunks(term):
        if chunks == 1:
            return term(0, slice(0, docs))

        def add(i, totals):
            terms = term(i, pl.ds(pl.multiple_of(i * chunk, chunk), chunk))
            return [total + one for total, one in zip(totals, terms)]

        return lax.fori_loop(0, chunks, add, [jnp.zeros((BLOCK, topics), F32) for _ in blocks])

    me = position()
    chain = docs // chains
    unit_rows = docs >> len(pairs)
    part_rows = unit_rows // chains

    def docs_of(i):
        place = lax.broadcasted_iota(jnp.int32, (1, chunk), 1) + i * chunk
        inside = lax.rem(place, chain)
        unit = unit_at(lax.div(inside, part_rows), me, pairs)
        return unit * unit_rows + lax.div(place, chain) * part_rows + lax.rem(inside, part_rows)

    def picked(i, docs_rows):
        hits = [(seeds_ref[rows, :] == docs_of(i)).astype(F32).astype(BF16) for rows in blocks]
        white = white_high[docs_rows, :]
        return [dot(hit, white, NN) for hit in hits]

    def moments(i, docs_rows):
        high, low = white_high[docs_rows, :], white_low[docs_rows, :]
        value = [dot(basis_high[rows, :], high, NT) + dot(basis_high[rows, :], low, NT) for rows in blocks]
        value = [split(v * v) for v in value]
        return [product(v, (high, low), NN) for v in value]

    def orthonormal(term, current):
        moment = over_chunks(term)
        norm = sum(jnp.sum(v * v, axis=0, keepdims=True) for v in moment)
        norm = jnp.sum(norm, axis=1, keepdims=True)
        scale = topics * jnp.sqrt(norm / (topics * topics) + EPS)
        start = SHIFT / (SHIFT + 1.0)
        weight = 1.0 / ((SHIFT + 1.0) * scale)
        for v, rows in zip(moment, blocks):
            value = v * weight + start * current(rows)
            basis[rows, :] = value
            basis_high[rows, :], basis_low[rows, :] = split(value)
        both = (basis_high[...], basis_low[...])
        cross = dot(both[0], both[1], NT)
        gram = dot(both[0], both[0], NT) + (cross + cross.T)
        gram = [gram[rows, :] for rows in blocks]
        diff = [diagonal(rows, start * start) - g for g, rows in zip(gram, blocks)]
        e = 1.0 - start * start
        q = 1.0
        for pair in range(SWEEPS // 2):
            for step in range(2):
                for d, rows in zip(diff, blocks):
                    diff_high[rows, :] = d.astype(BF16)
                whole = diff_high[...]
                second = [dot(diff_high[rows, :], whole, NN) for rows in blocks]
                if pair < SWEEPS // 2 - 1:
                    third = [dot(v.astype(BF16), whole, NN) for v in second]
                if step == 0:
                    c0, c1, c2, c3, c4 = series(e)
                    value = [c1 * diff[k] + c2 * second[k] for k in each]
                    for v, rows in zip(second, blocks):
                        square_high[rows, :] = v.astype(BF16)
                    square = square_high[...]
                    mixed = [(c3 * diff[k] + c4 * second[k]).astype(BF16) for k in each]
                    value = [value[k] + dot(mixed[k], square, NN) for k in each]
                    if pair == 0:
                        factor = value
                        for f, rows in zip(factor, blocks):
                            factor_high[rows, :] = f.astype(BF16)
                    else:
                        before = factor_high[...]
                        factor = [
                            q * value[k] + c0 * factor[k] + dot(value[k].astype(BF16), before, NN) for k in each
                        ]
                    q = q * c0
                if pair == SWEEPS // 2 - 1:
                    break
                e, c1, c2, c3 = following(e)
                diff = [c1 * diff[k] + c2 * second[k] + c3 * third[k] for k in each]
        parts = [split(f) for f in factor]
        value = [q * basis[rows, :] + product(parts[k], both, NN) for k, rows in enumerate(blocks)]
        for v, rows in zip(value, blocks):
            basis[rows, :] = v
            basis_high[rows, :], basis_low[rows, :] = split(v)

    orthonormal(picked, lambda rows: diagonal(rows, 1.0))

    for _ in range(ITERS):
        orthonormal(moments, lambda rows: basis[rows, :])
    parts = (basis_high[...], basis_low[...])
    total = jnp.zeros((1, topics), F32)
    for r in range(0, docs, chunk):
        value = product((white_high[r : r + chunk, :], white_low[r : r + chunk, :]), parts, NT)
        total += jnp.sum(value * value * value, axis=0, keepdims=True)
    weights_ref[...] = total / docs
    basis[...] = basis[...].T * math.sqrt(topics)
    own_rows = own_out.shape[0]
    own_out[...] = basis[pl.ds(pl.multiple_of(lax.axis_index("vocab") * own_rows, own_rows), own_rows), :]


def iterate(pieces, seeds, docs, pairs, own_rows):
    topics = seeds.shape[0]
    chunk = math.gcd(docs, 512)
    vmem = pl.BlockSpec(memory_space=pltpu.VMEM)
    return pl.pallas_call(
        functools.partial(iterate_kernel, chunk, pairs, CHAINS),
        in_specs=[vmem] * (1 + len(pieces)),
        out_specs=[vmem] * 2,
        out_shape=[
            jax.ShapeDtypeStruct((own_rows, topics), F32),
            jax.ShapeDtypeStruct((1, topics), F32),
        ],
        scratch_shapes=[
            pltpu.VMEM((topics, topics), F32),
            *[pltpu.VMEM((docs, topics), BF16)] * 2,
            *[pltpu.VMEM((topics, topics), BF16)] * 5,
        ],
        compiler_params=pltpu.CompilerParams(vmem_limit_bytes=40 << 20),
        name="iterate",
    )(seeds.reshape(topics, 1), *pieces)


CHAINS = 2
SCRATCH = 8
BLOCK = 256
VMEM_LIMIT = 53 << 20
CHUNKS = 4
AHEAD = 2
SWAP = True


def per_device(n_doc, n_vocab, count_tiles, tile_words, whitening, seeds):
    n = n_doc * n_vocab
    pairs, whole = plan(n_doc, n_vocab)
    halves = partial_rows(count_tiles[0], tile_words[0].T, whitening, pairs, CHAINS)
    rows, topics = halves[0].shape[0] * 2, whitening.shape[1]
    docs = rows * CHAINS
    values = [keep + exchange(send, pairs[0], n) for keep, send in zip(halves[::2], halves[1::2])]
    half = rows // 2
    for masks in pairs[1:]:
        half = half // 2
        values = [v[:half] + exchange(v[half:], masks, n) for v in values]
    for s in range(len(whole)):
        values = [v + exchange(v, whole[s ^ (c & 1) if SWAP else s], n) for c, v in enumerate(values)]
    for masks in reversed(pairs[2:]):
        values = [jnp.concatenate([v, exchange(v, masks, n)]) for v in values]
    pieces = []
    for v in values:
        rest = exchange(v, pairs[1], n)
        pieces += [v, rest, exchange(v, pairs[0], n), exchange(rest, pairs[0], n)]
    directions, weights = iterate(pieces, seeds, docs, pairs, topics // n_vocab)
    return directions, weights.reshape(topics)


def solution(mesh):
    in_specs = (
        P(("doc", "vocab"), None, None, None, None),
        P(("doc", "vocab"), None, None),
        P(("doc", "vocab"), None),
        P(),
    )
    out_specs = (P("vocab", None), P())
    return jax.shard_map(
        functools.partial(per_device, mesh.shape["doc"], mesh.shape["vocab"]),
        mesh=mesh,
        in_specs=in_specs,
        out_specs=out_specs,
        check_vma=False,
    )
```

```python
import functools
import math

import jax
import jax.numpy as jnp
from jax import lax
from jax.experimental import pallas as pl
from jax.experimental.pallas import tpu as pltpu
from jax.sharding import PartitionSpec as P

ITERS = 2
SWEEPS = 4
SHIFT = 2.0
EPS = 1e-06
AXES = ("doc", "vocab")
F32 = jnp.float32
BF16 = jnp.bfloat16
NN = (((1,), (0,)), ((), ()))
NT = (((1,), (1,)), ((), ()))


def split(value):
    high = value.astype(BF16)
    return high, (value - high.astype(F32)).astype(BF16)


def dot(left, right, dims):
    return lax.dot_general(left, right, dims, preferred_element_type=F32)


def product(left, right, dims):
    high = dot(left[0], right[0], dims)
    return high + (dot(left[0], right[1], dims) + dot(left[1], right[0], dims))


def plan(n_doc, n_vocab):
    n = n_doc * n_vocab
    bits = [1 << b for b in range(n.bit_length() - 1)]
    halving, whole = bits[:-2], bits[-2:]
    pairs = [(b, b) for b in halving]
    if len(halving) >= 3:
        pairs[1], pairs[2] = (halving[2], halving[1]), (halving[1], halving[2])
    return pairs, [(b, b) for b in whole]


def unit_at(place, me, pairs):
    steps = len(pairs)
    top = (place >> (steps - 1)) & 1
    odd = (me & 1) ^ top
    unit = (me & ((1 << steps) - 1)) ^ top
    for s in range(1, steps):
        even_mask, odd_mask = pairs[s]
        mask = even_mask + odd * (odd_mask - even_mask)
        unit = unit ^ (((place >> (steps - 1 - s)) & 1) * mask)
    return unit


def position():
    return lax.axis_index("doc") * lax.axis_size("vocab") + lax.axis_index("vocab")


def exchange(value, masks, n):
    perm = [(i, i ^ masks[i & 1]) for i in range(n)]
    return lax.ppermute(value, AXES, perm)


def whiten_kernel(pairs, unit_blocks, half_blocks, step_blocks, chains, words_in, tiles_in, table, *rest):
    outs, (words, dense, tiles, held, word_sem, tile_sem, sems) = rest[: 2 * chains], rest[2 * chains :]
    steps = half_blocks // step_blocks
    step = pl.program_id(0) if steps > 1 else 0
    me = position()
    doc_dev, word_block = tiles.shape[2], tiles.shape[3]
    chain_blocks = unit_blocks // chains
    chunk = held.shape[0] // CHUNKS
    cuts = [slice(k * chunk, (k + 1) * chunk) for k in range(CHUNKS)]
    fetch_words = pltpu.make_async_copy(words_in, words, word_sem)
    fetch_tiles = pltpu.make_async_copy(tiles_in, tiles, tile_sem)
    fetches = [pltpu.make_async_copy(table.at[cut], held.at[cut], sems.at[k]) for k, cut in enumerate(cuts)]

    def first(action):
        if steps > 1:
            pl.when(step == 0)(action)
        else:
            action()

    @first
    def _():
        fetch_words.start()
        fetch_tiles.start()
        for fetch in fetches[:AHEAD]:
            fetch.start()

    dense[...] = jnp.zeros_like(dense)
    first(fetch_words.wait)
    first(fetch_tiles.wait)
    for part in range(2 * chains):
        for inside in range(step_blocks):
            place = step * step_blocks + inside + (part % 2) * half_blocks
            unit = unit_at(place // chain_blocks, me, pairs)
            block = unit * unit_blocks + (part // 2) * chain_blocks + place % chain_blocks
            rows = pl.ds((part * step_blocks + inside) * doc_dev, doc_dev)
            for t in range(tiles.shape[1]):
                columns = pl.ds(pl.multiple_of(words[t, block] * word_block, word_block), word_block)
                dense[rows, columns] = dense[rows, columns] + tiles[block, t].astype(F32).astype(BF16)

    value = None
    for k, cut in enumerate(cuts):
        first(fetches[k].wait)
        if k + AHEAD < CHUNKS:
            first(fetches[k + AHEAD].start)
        term = dot(dense[:, cut], held[cut, :], NN)
        value = term if value is None else value + term
    rows = step_blocks * doc_dev
    for part in range(2 * chains):
        outs[part][...] = value[part * rows : (part + 1) * rows]


def partial_rows(tiles, words, table, pairs, chains):
    blocks, _, doc_dev, _ = tiles.shape
    topics = table.shape[1]
    unit_blocks = blocks >> len(pairs)
    half_blocks = blocks // 2 // chains
    step_blocks = math.gcd(half_blocks, 16 // chains)
    steps = half_blocks // step_blocks
    step_rows = step_blocks * doc_dev
    half = jax.ShapeDtypeStruct((half_blocks * doc_dev, topics), F32)
    if steps > 1:
        out = pl.BlockSpec((step_rows, topics), lambda i: (i, 0))
    else:
        out = pl.BlockSpec(memory_space=pltpu.VMEM)
    return pl.pallas_call(
        functools.partial(whiten_kernel, pairs, unit_blocks, half_blocks, step_blocks, chains),
        grid=(steps,) if steps > 1 else (),
        in_specs=[
            pl.BlockSpec(memory_space=pl.ANY),
            pl.BlockSpec(memory_space=pl.ANY),
            pl.BlockSpec(memory_space=pl.ANY),
        ],
        out_specs=[out] * (2 * chains),
        out_shape=[half] * (2 * chains),
        scratch_shapes=[
            pltpu.SMEM(words.shape, jnp.int32),
            pltpu.VMEM((2 * chains * step_rows, table.shape[0]), BF16),
            pltpu.VMEM(tiles.shape, jnp.int32),
            pltpu.VMEM(table.shape, BF16),
            pltpu.SemaphoreType.DMA,
            pltpu.SemaphoreType.DMA,
            pltpu.SemaphoreType.DMA((CHUNKS,)),
        ],
        compiler_params=pltpu.CompilerParams(vmem_limit_bytes=VMEM_LIMIT),
        name="whiten",
    )(words, tiles, table)


def series(e):
    return (
        1.0 + e / 2 + 0.375 * e**2 + 0.3125 * e**3 + 0.0625 * e**4,
        0.5 + 0.75 * e + 0.9375 * e**2 + 0.25 * e**3,
        0.375 + 0.9375 * e + 0.375 * e**2,
        0.3125 + 0.25 * e,
        0.0625,
    )


def following(e):
    return (3 * e**2 + e**3) / 4, (6 * e + 3 * e**2) / 4, (3 + 3 * e) / 4, 0.25


def iterate_kernel(chunk, pairs, chains, seeds_ref, *rest):
    refs, pieces = rest[-SCRATCH - 2 :], rest[: -SCRATCH - 2]
    own_out, weights_ref, basis, white_high, white_low, basis_high, basis_low, diff_high, factor_high, square_high = refs
    topics = basis.shape[0]
    docs = white_high.shape[0]
    chunks = docs // chunk
    blocks = [slice(r, r + BLOCK) for r in range(0, topics, BLOCK)]
    each = range(len(blocks))
    first = 0
    for piece in pieces:
        rows = slice(first, first + piece.shape[0])
        first = first + piece.shape[0]
        white_high[rows, :], white_low[rows, :] = split(piece[...])

    def diagonal(rows, value):
        row = lax.broadcasted_iota(jnp.int32, (BLOCK, topics), 0) + rows.start
        column = lax.broadcasted_iota(jnp.int32, (BLOCK, topics), 1)
        return jnp.where(row == column, value, 0.0).astype(F32)

    def over_chunks(term):
        if chunks == 1:
            return term(0, slice(0, docs))

        def add(i, totals):
            terms = term(i, pl.ds(pl.multiple_of(i * chunk, chunk), chunk))
            return [total + one for total, one in zip(totals, terms)]

        return lax.fori_loop(0, chunks, add, [jnp.zeros((BLOCK, topics), F32) for _ in blocks])

    me = position()
    chain = docs // chains
    unit_rows = docs >> len(pairs)
    part_rows = unit_rows // chains

    def docs_of(i):
        place = lax.broadcasted_iota(jnp.int32, (1, chunk), 1) + i * chunk
        inside = lax.rem(place, chain)
        unit = unit_at(lax.div(inside, part_rows), me, pairs)
        return unit * unit_rows + lax.div(place, chain) * part_rows + lax.rem(inside, part_rows)

    def picked(i, docs_rows):
        hits = [(seeds_ref[rows, :] == docs_of(i)).astype(F32).astype(BF16) for rows in blocks]
        white = white_high[docs_rows, :]
        return [dot(hit, white, NN) for hit in hits]

    def moments(i, docs_rows):
        high, low = white_high[docs_rows, :], white_low[docs_rows, :]
        value = [dot(basis_high[rows, :], high, NT) + dot(basis_high[rows, :], low, NT) for rows in blocks]
        value = [split(v * v) for v in value]
        return [product(v, (high, low), NN) for v in value]

    def orthonormal(term, first):
        moment = over_chunks(term)
        norm = sum(jnp.sum(v * v, axis=0, keepdims=True) for v in moment)
        norm = jnp.sum(norm, axis=1, keepdims=True)
        scale = topics * jnp.sqrt(norm / (topics * topics) + EPS)
        start = SHIFT / (SHIFT + 1.0)
        weight = 1.0 / ((SHIFT + 1.0) * scale)
        if first:
            for v, rows in zip(moment, blocks):
                basis[rows, :] = v
                basis_high[rows, :] = v.astype(BF16)
            both = (basis_high[...],)
            both_ways = basis[...] + basis[...].T
            gram = (start * weight) * both_ways + (weight * weight) * dot(both[0], both[0], NT)
            diff = [-gram[rows, :] for rows in blocks]
        else:
            for v, rows in zip(moment, blocks):
                value = v * weight + start * basis[rows, :]
                basis[rows, :] = value
                basis_high[rows, :], basis_low[rows, :] = split(value)
            both = (basis_high[...], basis_low[...])
            cross = dot(both[0], both[1], NT)
            gram = dot(both[0], both[0], NT) + (cross + cross.T)
            diff = [diagonal(rows, start * start) - gram[rows, :] for rows in blocks]
        e = 1.0 - start * start
        q = 1.0
        for pair in range(SWEEPS // 2):
            for step in range(2):
                for d, rows in zip(diff, blocks):
                    diff_high[rows, :] = d.astype(BF16)
                whole = diff_high[...]
                second = [dot(diff_high[rows, :], whole, NN) for rows in blocks]
                if pair < SWEEPS // 2 - 1:
                    third = [dot(v.astype(BF16), whole, NN) for v in second]
                if step == 0:
                    c0, c1, c2, c3, c4 = series(e)
                    value = [c1 * diff[k] + c2 * second[k] for k in each]
                    for v, rows in zip(second, blocks):
                        square_high[rows, :] = v.astype(BF16)
                    square = square_high[...]
                    mixed = [(c3 * diff[k] + c4 * second[k]).astype(BF16) for k in each]
                    value = [value[k] + dot(mixed[k], square, NN) for k in each]
                    if pair == 0:
                        factor = value
                        for f, rows in zip(factor, blocks):
                            factor_high[rows, :] = f.astype(BF16)
                    else:
                        before = factor_high[...]
                        factor = [
                            q * value[k] + c0 * factor[k] + dot(value[k].astype(BF16), before, NN) for k in each
                        ]
                    q = q * c0
                if pair == SWEEPS // 2 - 1:
                    break
                e, c1, c2, c3 = following(e)
                diff = [c1 * diff[k] + c2 * second[k] + c3 * third[k] for k in each]
        parts = [split(f) for f in factor]
        if first:
            value = [dot(parts[k][0], both[0], NN) + dot(parts[k][1], both[0], NN) for k in each]
            value = [
                weight * (value[k] + q * basis[rows, :]) + (start * factor[k] + diagonal(rows, q * start))
                for k, rows in enumerate(blocks)
            ]
        else:
            value = [q * basis[rows, :] + product(parts[k], both, NN) for k, rows in enumerate(blocks)]
        for v, rows in zip(value, blocks):
            basis[rows, :] = v
            basis_high[rows, :], basis_low[rows, :] = split(v)

    orthonormal(picked, True)

    for _ in range(ITERS):
        orthonormal(moments, False)
    parts = (basis_high[...], basis_low[...])
    total = jnp.zeros((1, topics), F32)
    for r in range(0, docs, chunk):
        value = product((white_high[r : r + chunk, :], white_low[r : r + chunk, :]), parts, NT)
        total += jnp.sum(value * value * value, axis=0, keepdims=True)
    weights_ref[...] = total / docs
    basis[...] = basis[...].T * math.sqrt(topics)
    own_rows = own_out.shape[0]
    own_out[...] = basis[pl.ds(pl.multiple_of(lax.axis_index("vocab") * own_rows, own_rows), own_rows), :]


def iterate(pieces, seeds, docs, pairs, own_rows):
    topics = seeds.shape[0]
    chunk = math.gcd(docs, 512)
    vmem = pl.BlockSpec(memory_space=pltpu.VMEM)
    return pl.pallas_call(
        functools.partial(iterate_kernel, chunk, pairs, CHAINS),
        in_specs=[vmem] * (1 + len(pieces)),
        out_specs=[vmem] * 2,
        out_shape=[
            jax.ShapeDtypeStruct((own_rows, topics), F32),
            jax.ShapeDtypeStruct((1, topics), F32),
        ],
        scratch_shapes=[
            pltpu.VMEM((topics, topics), F32),
            *[pltpu.VMEM((docs, topics), BF16)] * 2,
            *[pltpu.VMEM((topics, topics), BF16)] * 5,
        ],
        compiler_params=pltpu.CompilerParams(vmem_limit_bytes=40 << 20),
        name="iterate",
    )(seeds.reshape(topics, 1), *pieces)


CHAINS = 2
SCRATCH = 8
BLOCK = 256
VMEM_LIMIT = 53 << 20
CHUNKS = 4
AHEAD = 2
SWAP = True


def per_device(n_doc, n_vocab, count_tiles, tile_words, whitening, seeds):
    n = n_doc * n_vocab
    pairs, whole = plan(n_doc, n_vocab)
    halves = partial_rows(count_tiles[0], tile_words[0].T, whitening, pairs, CHAINS)
    rows, topics = halves[0].shape[0] * 2, whitening.shape[1]
    docs = rows * CHAINS
    values = [keep + exchange(send, pairs[0], n) for keep, send in zip(halves[::2], halves[1::2])]
    half = rows // 2
    for masks in pairs[1:]:
        half = half // 2
        values = [v[:half] + exchange(v[half:], masks, n) for v in values]
    for s in range(len(whole)):
        values = [v + exchange(v, whole[s ^ (c & 1) if SWAP else s], n) for c, v in enumerate(values)]
    for masks in reversed(pairs[2:]):
        values = [jnp.concatenate([v, exchange(v, masks, n)]) for v in values]
    pieces = []
    for v in values:
        rest = exchange(v, pairs[1], n)
        pieces += [v, rest, exchange(v, pairs[0], n), exchange(rest, pairs[0], n)]
    directions, weights = iterate(pieces, seeds, docs, pairs, topics // n_vocab)
    return directions, weights.reshape(topics)


def solution(mesh):
    in_specs = (
        P(("doc", "vocab"), None, None, None, None),
        P(("doc", "vocab"), None, None),
        P(("doc", "vocab"), None),
        P(),
    )
    out_specs = (P("vocab", None), P())
    return jax.shard_map(
        functools.partial(per_device, mesh.shape["doc"], mesh.shape["vocab"]),
        mesh=mesh,
        in_specs=in_specs,
        out_specs=out_specs,
        check_vma=False,
    )
```

```python
import functools
import math

import jax
import jax.numpy as jnp
from jax import lax
from jax.experimental import pallas as pl
from jax.experimental.pallas import tpu as pltpu
from jax.sharding import PartitionSpec as P

ITERS = 2
SWEEPS = 4
SHIFT = 2.0
EPS = 1e-06
AXES = ("doc", "vocab")
F32 = jnp.float32
BF16 = jnp.bfloat16
NN = (((1,), (0,)), ((), ()))
NT = (((1,), (1,)), ((), ()))


def split(value):
    high = value.astype(BF16)
    return high, (value - high.astype(F32)).astype(BF16)


def dot(left, right, dims):
    return lax.dot_general(left, right, dims, preferred_element_type=F32)


def product(left, right, dims):
    high = dot(left[0], right[0], dims)
    return high + (dot(left[0], right[1], dims) + dot(left[1], right[0], dims))


def plan(n_doc, n_vocab):
    n = n_doc * n_vocab
    bits = [1 << b for b in range(n.bit_length() - 1)]
    halving, whole = bits[:-2], bits[-2:]
    pairs = [(b, b) for b in halving]
    if len(halving) >= 3:
        pairs[1], pairs[2] = (halving[2], halving[1]), (halving[1], halving[2])
    return pairs, [(b, b) for b in whole]


def unit_at(place, me, pairs):
    steps = len(pairs)
    top = (place >> (steps - 1)) & 1
    odd = (me & 1) ^ top
    unit = (me & ((1 << steps) - 1)) ^ top
    for s in range(1, steps):
        even_mask, odd_mask = pairs[s]
        mask = even_mask + odd * (odd_mask - even_mask)
        unit = unit ^ (((place >> (steps - 1 - s)) & 1) * mask)
    return unit


def position():
    return lax.axis_index("doc") * lax.axis_size("vocab") + lax.axis_index("vocab")


def exchange(value, masks, n):
    perm = [(i, i ^ masks[i & 1]) for i in range(n)]
    return lax.ppermute(value, AXES, perm)


def whiten_kernel(pairs, unit_blocks, half_blocks, step_blocks, chains, words_in, tiles_in, table, *rest):
    outs, (words, dense, tiles, held, word_sem, tile_sem, sems) = rest[: 2 * chains], rest[2 * chains :]
    steps = half_blocks // step_blocks
    step = pl.program_id(0) if steps > 1 else 0
    me = position()
    doc_dev, word_block = tiles.shape[2], tiles.shape[3]
    chain_blocks = unit_blocks // chains
    chunk = held.shape[0] // CHUNKS
    cuts = [slice(k * chunk, (k + 1) * chunk) for k in range(CHUNKS)]
    fetch_words = pltpu.make_async_copy(words_in, words, word_sem)
    fetch_tiles = pltpu.make_async_copy(tiles_in, tiles, tile_sem)
    fetches = [pltpu.make_async_copy(table.at[cut], held.at[cut], sems.at[k]) for k, cut in enumerate(cuts)]

    def first(action):
        if steps > 1:
            pl.when(step == 0)(action)
        else:
            action()

    @first
    def _():
        fetch_words.start()
        fetch_tiles.start()
        for fetch in fetches[:AHEAD]:
            fetch.start()

    dense[...] = jnp.zeros_like(dense)
    first(fetch_words.wait)
    first(fetch_tiles.wait)
    for part in range(2 * chains):
        for inside in range(step_blocks):
            place = step * step_blocks + inside + (part % 2) * half_blocks
            unit = unit_at(place // chain_blocks, me, pairs)
            block = unit * unit_blocks + (part // 2) * chain_blocks + place % chain_blocks
            rows = pl.ds((part * step_blocks + inside) * doc_dev, doc_dev)
            for t in range(tiles.shape[1]):
                columns = pl.ds(pl.multiple_of(words[t, block] * word_block, word_block), word_block)
                dense[rows, columns] = dense[rows, columns] + tiles[block, t].astype(F32).astype(BF16)

    value = None
    for k, cut in enumerate(cuts):
        first(fetches[k].wait)
        if k + AHEAD < CHUNKS:
            first(fetches[k + AHEAD].start)
        term = dot(dense[:, cut], held[cut, :], NN)
        value = term if value is None else value + term
    rows = step_blocks * doc_dev
    for part in range(2 * chains):
        outs[part][...] = value[part * rows : (part + 1) * rows]


def partial_rows(tiles, words, table, pairs, chains):
    blocks, _, doc_dev, _ = tiles.shape
    topics = table.shape[1]
    unit_blocks = blocks >> len(pairs)
    half_blocks = blocks // 2 // chains
    step_blocks = math.gcd(half_blocks, 16 // chains)
    steps = half_blocks // step_blocks
    step_rows = step_blocks * doc_dev
    half = jax.ShapeDtypeStruct((half_blocks * doc_dev, topics), F32)
    if steps > 1:
        out = pl.BlockSpec((step_rows, topics), lambda i: (i, 0))
    else:
        out = pl.BlockSpec(memory_space=pltpu.VMEM)
    return pl.pallas_call(
        functools.partial(whiten_kernel, pairs, unit_blocks, half_blocks, step_blocks, chains),
        grid=(steps,) if steps > 1 else (),
        in_specs=[
            pl.BlockSpec(memory_space=pl.ANY),
            pl.BlockSpec(memory_space=pl.ANY),
            pl.BlockSpec(memory_space=pl.ANY),
        ],
        out_specs=[out] * (2 * chains),
        out_shape=[half] * (2 * chains),
        scratch_shapes=[
            pltpu.SMEM(words.shape, jnp.int32),
            pltpu.VMEM((2 * chains * step_rows, table.shape[0]), BF16),
            pltpu.VMEM(tiles.shape, jnp.int32),
            pltpu.VMEM(table.shape, BF16),
            pltpu.SemaphoreType.DMA,
            pltpu.SemaphoreType.DMA,
            pltpu.SemaphoreType.DMA((CHUNKS,)),
        ],
        compiler_params=pltpu.CompilerParams(vmem_limit_bytes=VMEM_LIMIT),
        name="whiten",
    )(words, tiles, table)


def series(e):
    return (
        1.0 + e / 2 + 0.375 * e**2 + 0.3125 * e**3 + 0.0625 * e**4,
        0.5 + 0.75 * e + 0.9375 * e**2 + 0.25 * e**3,
        0.375 + 0.9375 * e + 0.375 * e**2,
        0.3125 + 0.25 * e,
        0.0625,
    )


def following(e):
    return (3 * e**2 + e**3) / 4, (6 * e + 3 * e**2) / 4, (3 + 3 * e) / 4, 0.25


def iterate_kernel(chunk, pairs, chains, seeds_ref, *rest):
    refs, pieces = rest[-SCRATCH - 2 :], rest[: -SCRATCH - 2]
    own_out, weights_ref, basis, white_high, white_low, basis_high, basis_low, diff_high, factor_high, square_high = refs
    topics = basis.shape[0]
    docs = white_high.shape[0]
    chunks = docs // chunk
    blocks = [slice(r, r + BLOCK) for r in range(0, topics, BLOCK)]
    each = range(len(blocks))
    first = 0
    for piece in pieces:
        rows = slice(first, first + piece.shape[0])
        first = first + piece.shape[0]
        white_high[rows, :], white_low[rows, :] = split(piece[...])

    def diagonal(rows, value):
        row = lax.broadcasted_iota(jnp.int32, (BLOCK, topics), 0) + rows.start
        column = lax.broadcasted_iota(jnp.int32, (BLOCK, topics), 1)
        return jnp.where(row == column, value, 0.0).astype(F32)

    def over_chunks(term):
        if chunks == 1:
            return term(0, slice(0, docs))

        def add(i, totals):
            terms = term(i, pl.ds(pl.multiple_of(i * chunk, chunk), chunk))
            return [total + one for total, one in zip(totals, terms)]

        return lax.fori_loop(0, chunks, add, [jnp.zeros((BLOCK, topics), F32) for _ in blocks])

    me = position()
    chain = docs // chains
    unit_rows = docs >> len(pairs)
    part_rows = unit_rows // chains

    def docs_of(i):
        place = lax.broadcasted_iota(jnp.int32, (1, chunk), 1) + i * chunk
        inside = lax.rem(place, chain)
        unit = unit_at(lax.div(inside, part_rows), me, pairs)
        return unit * unit_rows + lax.div(place, chain) * part_rows + lax.rem(inside, part_rows)

    def picked(i, docs_rows):
        hits = [(seeds_ref[rows, :] == docs_of(i)).astype(F32).astype(BF16) for rows in blocks]
        white = white_high[docs_rows, :]
        return [dot(hit, white, NN) for hit in hits]

    def moments(i, docs_rows):
        high, low = white_high[docs_rows, :], white_low[docs_rows, :]
        value = [dot(basis_high[rows, :], high, NT) + dot(basis_high[rows, :], low, NT) for rows in blocks]
        value = [split(v * v) for v in value]
        return [product(v, (high, low), NN) for v in value]

    def orthonormal(term, first):
        moment = over_chunks(term)
        norm = sum(jnp.sum(v * v, axis=0, keepdims=True) for v in moment)
        norm = jnp.sum(norm, axis=1, keepdims=True)
        scale = topics * jnp.sqrt(norm / (topics * topics) + EPS)
        start = SHIFT / (SHIFT + 1.0)
        weight = 1.0 / ((SHIFT + 1.0) * scale)
        if first:
            for v, rows in zip(moment, blocks):
                basis[rows, :] = v
                basis_high[rows, :] = v.astype(BF16)
            both = (basis_high[...],)
            both_ways = basis[...] + both[0].T.astype(F32)
            gram = (start * weight) * both_ways + (weight * weight) * dot(both[0], both[0], NT)
            diff = [-gram[rows, :] for rows in blocks]
        else:
            for v, rows in zip(moment, blocks):
                value = v * weight + start * basis[rows, :]
                basis[rows, :] = value
                basis_high[rows, :], basis_low[rows, :] = split(value)
            both = (basis_high[...], basis_low[...])
            cross = dot(both[0], both[1], NT).astype(BF16)
            gram = dot(both[0], both[0], NT) + (cross.astype(F32) + cross.T.astype(F32))
            diff = [diagonal(rows, start * start) - gram[rows, :] for rows in blocks]
        e = 1.0 - start * start
        q = 1.0
        for pair in range(SWEEPS // 2):
            for step in range(2):
                for d, rows in zip(diff, blocks):
                    diff_high[rows, :] = d.astype(BF16)
                whole = diff_high[...]
                second = [dot(diff_high[rows, :], whole, NN) for rows in blocks]
                if pair < SWEEPS // 2 - 1:
                    third = [dot(v.astype(BF16), whole, NN) for v in second]
                if step == 0:
                    c0, c1, c2, c3, c4 = series(e)
                    value = [c1 * diff[k] + c2 * second[k] for k in each]
                    for v, rows in zip(second, blocks):
                        square_high[rows, :] = v.astype(BF16)
                    square = square_high[...]
                    mixed = [(c3 * diff[k] + c4 * second[k]).astype(BF16) for k in each]
                    value = [value[k] + dot(mixed[k], square, NN) for k in each]
                    if pair == 0:
                        factor = value
                        for f, rows in zip(factor, blocks):
                            factor_high[rows, :] = f.astype(BF16)
                    else:
                        before = factor_high[...]
                        factor = [
                            q * value[k] + c0 * factor[k] + dot(value[k].astype(BF16), before, NN) for k in each
                        ]
                    q = q * c0
                if pair == SWEEPS // 2 - 1:
                    break
                e, c1, c2, c3 = following(e)
                diff = [c1 * diff[k] + c2 * second[k] + c3 * third[k] for k in each]
        parts = [split(f) for f in factor]
        if first:
            value = [dot(parts[k][0], both[0], NN) + dot(parts[k][1], both[0], NN) for k in each]
            value = [
                weight * (value[k] + q * basis[rows, :]) + (start * factor[k] + diagonal(rows, q * start))
                for k, rows in enumerate(blocks)
            ]
        else:
            value = [q * basis[rows, :] + product(parts[k], both, NN) for k, rows in enumerate(blocks)]
        for v, rows in zip(value, blocks):
            basis[rows, :] = v
            basis_high[rows, :], basis_low[rows, :] = split(v)

    orthonormal(picked, True)

    for _ in range(ITERS):
        orthonormal(moments, False)
    parts = (basis_high[...], basis_low[...])
    total = jnp.zeros((1, topics), F32)
    for r in range(0, docs, chunk):
        value = product((white_high[r : r + chunk, :], white_low[r : r + chunk, :]), parts, NT)
        total += jnp.sum(value * value * value, axis=0, keepdims=True)
    weights_ref[...] = total / docs
    own_rows = own_out.shape[0]
    own = pl.ds(pl.multiple_of(lax.axis_index("vocab") * own_rows, own_rows), own_rows)
    if own_rows % 128 == 0:
        own_out[...] = basis[:, own].T * math.sqrt(topics)
    else:
        basis[...] = basis[...].T * math.sqrt(topics)
        own_out[...] = basis[own, :]


def iterate(pieces, seeds, docs, pairs, own_rows):
    topics = seeds.shape[0]
    chunk = math.gcd(docs, 512)
    vmem = pl.BlockSpec(memory_space=pltpu.VMEM)
    return pl.pallas_call(
        functools.partial(iterate_kernel, chunk, pairs, CHAINS),
        in_specs=[vmem] * (1 + len(pieces)),
        out_specs=[vmem] * 2,
        out_shape=[
            jax.ShapeDtypeStruct((own_rows, topics), F32),
            jax.ShapeDtypeStruct((1, topics), F32),
        ],
        scratch_shapes=[
            pltpu.VMEM((topics, topics), F32),
            *[pltpu.VMEM((docs, topics), BF16)] * 2,
            *[pltpu.VMEM((topics, topics), BF16)] * 5,
        ],
        compiler_params=pltpu.CompilerParams(vmem_limit_bytes=40 << 20),
        name="iterate",
    )(seeds.reshape(topics, 1), *pieces)


CHAINS = 2
SCRATCH = 8
BLOCK = 256
VMEM_LIMIT = 53 << 20
CHUNKS = 4
AHEAD = 2
SWAP = True


def per_device(n_doc, n_vocab, count_tiles, tile_words, whitening, seeds):
    n = n_doc * n_vocab
    pairs, whole = plan(n_doc, n_vocab)
    halves = partial_rows(count_tiles[0], tile_words[0].T, whitening, pairs, CHAINS)
    rows, topics = halves[0].shape[0] * 2, whitening.shape[1]
    docs = rows * CHAINS
    values = [keep + exchange(send, pairs[0], n) for keep, send in zip(halves[::2], halves[1::2])]
    half = rows // 2
    for masks in pairs[1:]:
        half = half // 2
        values = [v[:half] + exchange(v[half:], masks, n) for v in values]
    for s in range(len(whole)):
        values = [v + exchange(v, whole[s ^ (c & 1) if SWAP else s], n) for c, v in enumerate(values)]
    for masks in reversed(pairs[2:]):
        values = [jnp.concatenate([v, exchange(v, masks, n)]) for v in values]
    pieces = []
    for v in values:
        rest = exchange(v, pairs[1], n)
        pieces += [v, rest, exchange(v, pairs[0], n), exchange(rest, pairs[0], n)]
    directions, weights = iterate(pieces, seeds, docs, pairs, topics // n_vocab)
    return directions, weights.reshape(topics)


def solution(mesh):
    in_specs = (
        P(("doc", "vocab"), None, None, None, None),
        P(("doc", "vocab"), None, None),
        P(("doc", "vocab"), None),
        P(),
    )
    out_specs = (P("vocab", None), P())
    return jax.shard_map(
        functools.partial(per_device, mesh.shape["doc"], mesh.shape["vocab"]),
        mesh=mesh,
        in_specs=in_specs,
        out_specs=out_specs,
        check_vma=False,
    )
```
